32 devices in a mesh: groups: 2 (over y), grid: 4 (over z), col: 2 (over x), sub: 2 (over core).
Axes of the slice: x: 2, y: 2, z: 4, core: 2. Of those that a mesh axis runs over, the one named last changes fastest.
Arguments:
- tokens: bfloat16 [512, 8192], P(('groups', 'grid'), ('col', 'sub')), parts along dimension 0, may hold values from -6 to 6
- teacher_gate: bfloat16 [14336, 8192], P('grid', ('col', 'sub')), may hold values from -0.0625 to 0.0625
- teacher_up: bfloat16 [14336, 8192], P('grid', ('col', 'sub')), may hold values from -0.0625 to 0.0625
- student_gate: bfloat16 [14336, 8192], P('grid', ('col', 'sub')), may hold values from -0.0625 to 0.0625
- student_up: bfloat16 [14336, 8192], P('grid', ('col', 'sub')), may hold values from -0.0625 to 0.0625
- keep_gate: int32 [112, 64], P('grid'), may hold values from -1 to 63, as said below
- keep_up: int32 [112, 64], P('grid'), may hold values from -1 to 63, as said below
Outputs:
- grad_gate: bfloat16 [28672, 8192], P(('groups', 'grid'), ('col', 'sub')), parts along dimension 0
- grad_up: bfloat16 [28672, 8192], P(('groups', 'grid'), ('col', 'sub')), parts along dimension 0
The draws below stay inside these ranges and needn't reach their ends.
There are 2 independent parts, one for each index of `groups`. The reference program is written for one: setup_inputs(seed, part) draws one part's arguments, and reference() takes and returns one part's arrays. A program takes and returns all parts, laid end to end along the dimension named above; an argument that names none is the same for every part. Nothing has to cross between parts.
Inputs may be any that keep to these rules, and one draw needn't show every extreme that they name: `keep_gate`: each row lists distinct column-block numbers in rising order, then -1 to the end of the row; each row keeps at least (201) // 10 and at most 57 blocks, and some row keeps each of these two counts. `keep_up`: each row lists distinct column-block numbers in rising order, then -1 to the end of the row; each row keeps at least (201) // 10 and at most 57 blocks, and some row keeps each of these two counts.
All inputs are finite; a program needn't handle non-finite values.
Results may differ from the reference program's by a relative error of at most 0.025.
Values may be sent and summed in bfloat16 or wider, within the bound.
No kernel may reach another device: no remote copies, remote signals or barrier semaphores. Data moves between devices by JAX's collectives and lax.ppermute only.
A program may use at most 256 MiB of HBM per device.

```python
import jax
import jax.numpy as jnp
from jax import lax

D = 8192
FF = 14336
BLOCK = 128
TOKENS = 256
PIECES = 4
FB = 112
DB = 64


def draw_lists(base):
    key_count, key_slot, key_order = jax.random.split(base, 3)
    lowest = (3 * DB + 9) // 10
    highest = 9 * DB // 10
    counts = jax.random.randint(key_count, (FB,), lowest, highest + 1)
    slots = jax.random.permutation(key_slot, FB)
    counts = jnp.where(slots == 0, lowest, jnp.where(slots == 1, highest, counts))
    scores = jax.random.randint(key_order, (FB, DB), 0, 1 << 20) * DB + jnp.arange(DB, dtype=jnp.int32)[None, :]
    order = jnp.argsort(scores, axis=1).astype(jnp.int32)
    position = jnp.arange(DB, dtype=jnp.int32)[None, :]
    chosen = jnp.where(position < counts[:, None], order, DB)
    ranked = jnp.sort(chosen, axis=1)
    return jnp.where(ranked >= DB, -1, ranked).astype(jnp.int32)


def draw_keep_gate(key, part):
    key = jax.random.fold_in(key, 5)
    return draw_lists(key)


def draw_keep_up(key, part):
    key = jax.random.fold_in(key, 9)
    return draw_lists(key)


def block_levels(stream_key, dims, cuts, smallest, largest):
    gain = 1.0
    for dim, parts in cuts:
        heights = jax.random.uniform(jax.random.fold_in(jax.random.fold_in(stream_key, 6), dim), (parts,), jnp.float32, smallest / len(cuts), largest / len(cuts))
        gain = gain * jnp.repeat(jnp.exp(heights), dims[dim] // parts).reshape((-1,) + (1,) * (len(dims) - 1 - dim))
    return gain


def normal_values(rng, dims, spread, bound, cuts=(), held_as=jnp.bfloat16):
    factor_of = block_levels(rng, dims, cuts, -0.22, 0.18) if cuts else 1.0
    entries = jax.random.normal(rng, dims, jnp.float32) * spread * factor_of
    return jnp.minimum(jnp.maximum(entries, -bound), bound).astype(held_as)


def setup_inputs(seed: int = 0, part: int = 0) -> dict:
    streams_of = jax.random.split(jax.random.key(seed), 8)
    part_keys = jax.random.split(jax.random.fold_in(streams_of[7], part), 8)
    tokens = normal_values(part_keys[0], (TOKENS, D), 1.0, 6.0, ((0, 4), (1, 4)))
    teacher_gate = normal_values(streams_of[1], (FF, D), D ** -0.5, 0.0625, ((0, 4), (1, 4)))
    teacher_up = normal_values(streams_of[2], (FF, D), D ** -0.5, 0.0625, ((0, 4), (1, 4)))
    student_gate = normal_values(streams_of[3], (FF, D), D ** -0.5, 0.0625, ((0, 4), (1, 4)))
    student_up = normal_values(streams_of[4], (FF, D), D ** -0.5, 0.0625, ((0, 4), (1, 4)))
    keep_gate = draw_keep_gate(jax.random.fold_in(streams_of[7], 71), part)
    keep_up = draw_keep_up(jax.random.fold_in(streams_of[7], 71), part)
    return {"tokens": tokens, "teacher_gate": teacher_gate, "teacher_up": teacher_up, "student_gate": student_gate, "student_up": student_up, "keep_gate": keep_gate, "keep_up": keep_up}


def expand_mask(keep):
    rows_count = keep.shape[0]
    cols_count = keep.shape[1]
    col_ids = jnp.arange(cols_count, dtype=jnp.int32)
    blocks = jnp.any(keep[:, :, None] == col_ids[None, None, :], axis=1)
    tiles = jnp.broadcast_to(blocks[:, None, :, None], (rows_count, BLOCK, cols_count, BLOCK))
    return tiles.reshape(rows_count * BLOCK, cols_count * BLOCK).astype(jnp.bfloat16)


def preact(tokens, weight):
    span = D // PIECES
    total = jnp.zeros((tokens.shape[0], weight.shape[0]), jnp.float32)
    for piece_index in range(PIECES):
        left = tokens[:, piece_index * span:(piece_index + 1) * span]
        right = weight[:, piece_index * span:(piece_index + 1) * span]
        partial_sum = jnp.dot(left, right.T, preferred_element_type=jnp.float32)
        rounded = lax.optimization_barrier(partial_sum.astype(jnp.bfloat16))
        total = total + rounded.astype(jnp.float32)
    return total


def reference(tokens, teacher_gate, teacher_up, student_gate, student_up, keep_gate, keep_up):
    mask_gate = expand_mask(keep_gate)
    mask_up = expand_mask(keep_up)
    pruned_gate = student_gate * mask_gate
    pruned_up = student_up * mask_up
    teacher_g = preact(tokens, teacher_gate)
    teacher_u = preact(tokens, teacher_up)
    student_g = preact(tokens, pruned_gate)
    student_u = preact(tokens, pruned_up)
    sigma_s = jax.nn.sigmoid(student_g)
    sigma_t = jax.nn.sigmoid(teacher_g)
    diff = student_g * sigma_s * student_u - teacher_g * sigma_t * teacher_u
    d_gate = (diff * student_u * sigma_s * (1.0 + student_g * (1.0 - sigma_s))).astype(jnp.bfloat16)
    d_up = (diff * student_g * sigma_s).astype(jnp.bfloat16)
    grad_gate = jnp.dot(d_gate.T, tokens, preferred_element_type=jnp.float32) * mask_gate
    grad_up = jnp.dot(d_up.T, tokens, preferred_element_type=jnp.float32) * mask_up
    return grad_gate.astype(jnp.bfloat16), grad_up.astype(jnp.bfloat16)
```

```python
import functools
import math

import jax
import jax.numpy as jnp
from jax import lax
from jax.experimental import pallas as pl
from jax.experimental.pallas import tpu as pltpu
from jax.sharding import PartitionSpec as P

BLOCK = 128
SLOTS = 6
OUT_SLOTS = 4
PARTS = (2, 3, 2)
ORDER = ("F0", "S0", "F1+", "D0+", "S1", "F2+", "R0", "D1", "G0+", "S2", "R1", "G1", "D2", "R2", "G2")
HBM = pl.BlockSpec(memory_space=pltpu.HBM)
ANY = pl.BlockSpec(memory_space=pl.ANY)
VM = pl.BlockSpec(memory_space=pltpu.VMEM)
SM = pl.BlockSpec(memory_space=pltpu.SMEM)
LONG = pl.CostEstimate(flops=2 * 10**10, bytes_accessed=1, transcendentals=0)
SHORT = pl.CostEstimate(flops=1, bytes_accessed=1, transcendentals=0)


def params(mib):
    return pltpu.CompilerParams(vmem_limit_bytes=mib * 2**20)


def mask_rows(keep_rows, first_block, block_count, group):
    col_ids = first_block + jnp.arange(block_count, dtype=jnp.int32)
    blocks = jnp.any(keep_rows[:, :, None] == col_ids[None, None, :], axis=1).astype(jnp.float32)
    blocks = jnp.repeat(blocks, BLOCK // group, axis=0)
    return jnp.repeat(blocks, BLOCK, axis=1)[:, None, :]


def forward_kernel(g, first, nx, nq, where, tok, mg, mu, w0, w1, w2, w3, *rest):
    sib, own, buf, held, sem, out_sem = rest[-6:]
    weights, masks = (w0, w1, w2, w3), (mg, mu)
    depth = tok.shape[1]
    steps = 2 * nx * nq

    def offset_of(part):
        return lax.rem(lax.rem(part, nx) + 1, nx)

    def group_of(i):
        part = i // nq
        side = lax.rem(where[0] + 1 + part // nx, 2)
        piece = lax.rem(where[1] + offset_of(part), nx)
        return first + (side * nx + piece) * nq + lax.rem(i, nq)

    def copies(i):
        slot = lax.rem(i, SLOTS)
        start = pl.multiple_of(group_of(i) * g, g)
        return [
            pltpu.make_async_copy(weights[m].at[pl.ds(start, g)], buf.at[slot, m], sem.at[slot, m]) for m in range(4)
        ]

    def start_all(i):
        for copy in copies(i):
            copy.start()

    pl.loop(0, min(SLOTS - 1, steps))(start_all)

    @pl.loop(0, steps)
    def _(i):
        slot = lax.rem(i, SLOTS)
        for copy in copies(i):
            copy.wait()
        pl.when(i + SLOTS - 1 < steps)(lambda: start_all(i + SLOTS - 1))
        for m in (2, 3):
            buf[slot, m] = buf[slot, m] * masks[m - 2][group_of(i)].astype(jnp.bfloat16)
        sums = lax.dot_general(
            buf[slot].reshape(4 * g, depth), tok[...], (((1,), (1,)), ((), ())), preferred_element_type=jnp.float32
        ).astype(jnp.bfloat16)
        part = i // nq
        rows = pl.ds(pl.multiple_of(lax.rem(i, nq) * g, g), g)
        for m in range(4):
            held[part, m, rows] = sums[m * g : (m + 1) * g]

        @pl.when(lax.rem(i, nq) == nq - 1)
        def _():
            @pl.when(part < nx)
            def _():
                pltpu.make_async_copy(held.at[part], sib.at[offset_of(part)], out_sem.at[part]).start()

            @pl.when(part >= nx)
            def _():
                pltpu.make_async_copy(held.at[part], own.at[offset_of(part)], out_sem.at[part]).start()

    for part in range(2 * nx):
        target = sib if part < nx else own
        pltpu.make_async_copy(held.at[part], target.at[(part % nx + 1) % nx], out_sem.at[part]).wait()


def forward_call(g, first, nx, nq, where, tok, masks, weights, after, cost):
    count, depth = tok.shape
    rows = 2 * nx * nq * g
    shape = jax.ShapeDtypeStruct((nx, 4, nq * g, count), jnp.bfloat16)
    return pl.pallas_call(
        functools.partial(forward_kernel, g, first, nx, nq),
        in_specs=[SM, VM, VM, VM] + [HBM] * 4 + [ANY] * len(after),
        out_specs=(ANY, ANY),
        out_shape=(shape, shape),
        scratch_shapes=[
            pltpu.VMEM((SLOTS, 4, g, depth), jnp.bfloat16),
            pltpu.VMEM((2 * nx, 4, nq * g, count), jnp.bfloat16),
            pltpu.SemaphoreType.DMA((SLOTS, 4)),
            pltpu.SemaphoreType.DMA((2 * nx,)),
        ],
        compiler_params=params(44),
        cost_estimate=cost,
        name="forward",
    )(where, tok, *masks, *weights, *after)


def sum_kernel(count, *refs):
    own, got = refs[0], refs[1]
    outs = refs[-count:]
    for k, out in enumerate(outs):
        out[...] = (own[k + 1].astype(jnp.float32) + got[k + 1].astype(jnp.float32)).astype(jnp.bfloat16)


def sum_call(nx, own, got, after):
    shape = own.shape[1:]
    step = min(64, shape[1])
    block = pl.BlockSpec((nx,) + (4, step, shape[2]), lambda i: (0, 0, i, 0))
    out_block = pl.BlockSpec((4, step, shape[2]), lambda i: (0, i, 0))
    size = math.prod(shape)
    return pl.pallas_call(
        functools.partial(sum_kernel, nx - 1),
        grid=(shape[1] // step,),
        in_specs=[block, block] + [ANY] * len(after),
        out_specs=[out_block] * (nx - 1),
        out_shape=[jax.ShapeDtypeStruct(shape, jnp.bfloat16)] * (nx - 1),
        compiler_params=params(16),
        cost_estimate=SHORT,
        name="sums",
    )(own, got, *after)


def delta_kernel(count, own, got, *refs):
    arrived, out = refs[:count], refs[-1]

    def total(m):
        value = own[0, m].astype(jnp.float32) + got[0, m].astype(jnp.float32)
        for ref in arrived:
            value = value + ref[m].astype(jnp.float32)
        return value

    teacher_g, teacher_u, student_g, student_u = total(0), total(1), total(2), total(3)
    sigma_s = jax.nn.sigmoid(student_g)
    sigma_t = jax.nn.sigmoid(teacher_g)
    diff = student_g * sigma_s * student_u - teacher_g * sigma_t * teacher_u
    out[0] = (diff * student_u * sigma_s * (1.0 + student_g * (1.0 - sigma_s))).astype(jnp.bfloat16)
    out[1] = (diff * student_g * sigma_s).astype(jnp.bfloat16)


def delta_call(nx, own, got, arrived, after, cost):
    rows, count = own.shape[2:]
    step = min(64, rows)
    first = pl.BlockSpec((1, 4, step, count), lambda i: (0, 0, i, 0))
    other = pl.BlockSpec((4, step, count), lambda i: (0, i, 0))
    return pl.pallas_call(
        functools.partial(delta_kernel, nx - 1),
        grid=(rows // step,),
        in_specs=[first, first] + [other] * (nx - 1) + [ANY] * len(after),
        out_specs=pl.BlockSpec((2, step, count), lambda i: (0, i, 0)),
        out_shape=jax.ShapeDtypeStruct((2, rows, count), jnp.bfloat16),
        compiler_params=params(16),
        cost_estimate=cost,
        name="deltas",
    )(own, got, *arrived, *after)


def relay_kernel(count, *refs):
    for source, target in zip(refs[:count], refs[-count:]):
        target[...] = source[...]


def relay_call(pieces, after):
    count = len(pieces)
    return pl.pallas_call(
        functools.partial(relay_kernel, count),
        in_specs=[VM] * count + [ANY] * len(after),
        out_specs=[VM] * count,
        out_shape=[jax.ShapeDtypeStruct(x.shape, x.dtype) for x in pieces],
        compiler_params=params(16),
        cost_estimate=SHORT,
        name="relay",
    )(*pieces, *after)


def grads_kernel(g, first, nx, nq, count, width, where, tok, mg, mu, *refs):
    deltas = refs[:count]
    gate, up, _, left, buf, in_sem, out_sem = refs[-7:]
    masks, outs = (mg, mu), (gate, up)
    rows = nq * g
    steps = 2 * (tok.shape[1] // width)
    arrivals = [pltpu.make_async_copy(deltas[b], left.at[:, b], in_sem.at[b]) for b in range(count)]
    for copy in arrivals:
        copy.start()

    groups = []
    for b in range(count):
        side = lax.rem(where[0] + b // nx, 2)
        groups.append(first + (side * nx + lax.rem(where[1] + nx - b % nx, nx)) * nq)

    def columns(t):
        return pl.ds(pl.multiple_of((t // 2) * width, width), width)

    def leave(t, m):
        slot = lax.rem(t, OUT_SLOTS)
        return [
            pltpu.make_async_copy(
                buf.at[slot, b],
                outs[m].at[pl.ds(pl.multiple_of(groups[b] * g, g), rows), columns(t)],
                out_sem.at[slot, b],
            )
            for b in range(count)
        ]

    for copy in arrivals:
        copy.wait()

    @pl.loop(0, steps)
    def _(t):
        slot, m, cols = lax.rem(t, OUT_SLOTS), lax.rem(t, 2), columns(t)

        @pl.when(t >= OUT_SLOTS)
        def _():
            for copy in leave(t - OUT_SLOTS, 0):
                copy.wait()

        sums = jnp.dot(
            left[m].reshape(count * rows, left.shape[3]), tok[:, cols], preferred_element_type=jnp.float32
        ).astype(jnp.bfloat16)
        for b in range(count):
            for r in range(nq):
                gate_row = masks[0][groups[b] + r, :, cols]
                up_row = masks[1][groups[b] + r, :, cols]
                row = jnp.where(m == 0, gate_row, up_row).astype(jnp.bfloat16)
                at = b * rows + r * g
                buf[slot, b, r * g : (r + 1) * g] = sums[at : at + g] * row
        for which in range(2):

            @pl.when(m == which)
            def _():
                for copy in leave(t, which):
                    copy.start()

    for t in range(max(0, steps - OUT_SLOTS), steps):
        for copy in leave(t, t % 2):
            copy.wait()


def grads_call(g, first, nx, nq, where, tok, masks, deltas, grads, shape, after, cost):
    tokens, depth = tok.shape
    rows = nq * g
    count = len(deltas)
    width = min(512, depth)
    held = [] if grads is None else list(grads)
    base = 4 + count
    grad = jax.ShapeDtypeStruct(shape, jnp.bfloat16)
    return pl.pallas_call(
        functools.partial(grads_kernel, g, first, nx, nq, count, width),
        in_specs=[SM, VM, VM, VM] + [ANY] * count + [HBM] * len(held) + [ANY] * len(after),
        out_specs=(HBM, HBM, ANY),
        out_shape=(grad, grad, jax.ShapeDtypeStruct((8, BLOCK), jnp.float32)),
        scratch_shapes=[
            pltpu.VMEM((2, count, rows, tokens), jnp.bfloat16),
            pltpu.VMEM((OUT_SLOTS, count, rows, width), jnp.bfloat16),
            pltpu.SemaphoreType.DMA((count,)),
            pltpu.SemaphoreType.DMA((OUT_SLOTS, count)),
        ],
        input_output_aliases={base: 0, base + 1: 1} if held else {},
        compiler_params=params(44),
        cost_estimate=cost,
        name="grads",
    )(where, tok, *masks, *deltas, *held, *after)


def per_device(nx, nz, tokens, teacher_gate, teacher_up, student_gate, student_up, keep_gate, keep_up):
    local_ff, local_d = student_gate.shape
    g = math.gcd(local_ff // (2 * nx), BLOCK)
    block_count = local_d // BLOCK
    first_block = lax.axis_index(("col", "sub")) * block_count
    masks = [mask_rows(keep, first_block, block_count, g) for keep in (keep_gate, keep_up)]
    weights = (teacher_gate, teacher_up, student_gate, student_up)
    where = jnp.stack([lax.axis_index("sub"), lax.axis_index("col")]).astype(jnp.int32)

    def swap(x):
        return lax.ppermute(x, "sub", [(0, 1), (1, 0)])

    def turn(x, k):
        return lax.ppermute(x, "col", [(i, (i + k) % nx) for i in range(nx)])

    if nz == 4:
        others = [lax.ppermute(tokens, "grid", [(i, i ^ k) for i in range(nz)]) for k in (1, 2, 3)]
        tok = jnp.concatenate([tokens] + others, axis=0)
    else:
        tok = lax.all_gather(tokens, "grid", axis=0, tiled=True)

    total = local_ff // (2 * nx * g)
    if sum(PARTS) == total:
        parts, order = PARTS, ORDER
    else:
        parts = (1,) * total
        order = [kind + str(u) for u in range(total) for kind in "FSDRG"]
    grads = None
    units = [(sum(parts[:u]) * 2 * nx, nq) for u, nq in enumerate(parts)]
    state = {}
    after = ()
    for step in order:
        kind, u = step[0], int(step[1])
        cost = LONG if step.endswith("+") else SHORT
        first, nq = units[u]
        if kind == "F":
            sib, own = forward_call(g, first, nx, nq, where, tok, masks, weights, after, cost)
            state[u] = (own, swap(sib))
            after = (own,)
        elif kind == "S":
            own, got = state[u]
            sends = sum_call(nx, own, got, after)
            state[u] = (own, got, [turn(sends[k - 1], k) for k in range(1, nx)])
            after = (sends[0],)
        elif kind == "D":
            own, got, arrived = state[u]
            mine = delta_call(nx, own, got, arrived, after, cost)
            state[u] = ([mine, swap(mine)], [turn(mine, k) for k in range(1, nx)])
            after = (mine,)
        elif kind == "R":
            (mine, theirs), far = state[u]
            near = relay_call(far, after)
            state[u] = [mine, *near, theirs, *[swap(x) for x in near]]
            after = (near[0],)
        else:
            *grads, done = grads_call(
                g, first, nx, nq, where, tok, masks, state[u], grads, (local_ff, local_d), after, cost
            )
            after = (done,)
    return tuple(grads)


def solution(mesh):
    return jax.shard_map(
        functools.partial(per_device, mesh.shape["col"], mesh.shape["grid"]),
        mesh=mesh,
        in_specs=(
            P(("groups", "grid"), ("col", "sub")),
            P("grid", ("col", "sub")),
            P("grid", ("col", "sub")),
            P("grid", ("col", "sub")),
            P("grid", ("col", "sub")),
            P("grid", None),
            P("grid", None),
        ),
        out_specs=(P(("groups", "grid"), ("col", "sub")), P(("groups", "grid"), ("col", "sub"))),
        check_vma=False,
    )
```

```python
import functools
import math

import jax
import jax.numpy as jnp
from jax import lax
from jax.experimental import pallas as pl
from jax.experimental.pallas import tpu as pltpu
from jax.sharding import PartitionSpec as P

BLOCK = 128
SLOTS = 6
OUT_SLOTS = 4
PARTS = (2, 3, 2)
ORDER = ("F0", "S0", "F1+", "D0+", "S1", "F2+", "R0", "D1", "G0+", "S2", "R1", "G1", "D2", "H2", "R2", "K2")
HBM = pl.BlockSpec(memory_space=pltpu.HBM)
ANY = pl.BlockSpec(memory_space=pl.ANY)
VM = pl.BlockSpec(memory_space=pltpu.VMEM)
SM = pl.BlockSpec(memory_space=pltpu.SMEM)
LONG = pl.CostEstimate(flops=2 * 10**10, bytes_accessed=1, transcendentals=0)
SHORT = pl.CostEstimate(flops=1, bytes_accessed=1, transcendentals=0)


def params(mib):
    return pltpu.CompilerParams(vmem_limit_bytes=mib * 2**20)


def mask_rows(keep_rows, first_block, block_count, group):
    col_ids = first_block + jnp.arange(block_count, dtype=jnp.int32)
    blocks = jnp.any(keep_rows[:, :, None] == col_ids[None, None, :], axis=1).astype(jnp.float32)
    blocks = jnp.repeat(blocks, BLOCK // group, axis=0)
    return jnp.repeat(blocks, BLOCK, axis=1)[:, None, :]


def forward_kernel(g, first, nx, nq, where, tok, mg, mu, w0, w1, w2, w3, *rest):
    sib, own, buf, held, sem, out_sem = rest[-6:]
    weights, masks = (w0, w1, w2, w3), (mg, mu)
    depth = tok.shape[1]
    steps = 2 * nx * nq

    def offset_of(part):
        return lax.rem(lax.rem(part, nx) + 1, nx)

    def group_of(i):
        part = i // nq
        side = lax.rem(where[0] + 1 + part // nx, 2)
        piece = lax.rem(where[1] + offset_of(part), nx)
        return first + (side * nx + piece) * nq + lax.rem(i, nq)

    def copies(i):
        slot = lax.rem(i, SLOTS)
        start = pl.multiple_of(group_of(i) * g, g)
        return [
            pltpu.make_async_copy(weights[m].at[pl.ds(start, g)], buf.at[slot, m], sem.at[slot, m]) for m in range(4)
        ]

    def start_all(i):
        for copy in copies(i):
            copy.start()

    pl.loop(0, min(SLOTS - 1, steps))(start_all)

    @pl.loop(0, steps)
    def _(i):
        slot = lax.rem(i, SLOTS)
        for copy in copies(i):
            copy.wait()
        pl.when(i + SLOTS - 1 < steps)(lambda: start_all(i + SLOTS - 1))
        for m in (2, 3):
            buf[slot, m] = buf[slot, m] * masks[m - 2][group_of(i)].astype(jnp.bfloat16)
        sums = lax.dot_general(
            buf[slot].reshape(4 * g, depth), tok[...], (((1,), (1,)), ((), ())), preferred_element_type=jnp.float32
        ).astype(jnp.bfloat16)
        part = i // nq
        rows = pl.ds(pl.multiple_of(lax.rem(i, nq) * g, g), g)
        for m in range(4):
            held[part, m, rows] = sums[m * g : (m + 1) * g]

        @pl.when(lax.rem(i, nq) == nq - 1)
        def _():
            @pl.when(part < nx)
            def _():
                pltpu.make_async_copy(held.at[part], sib.at[offset_of(part)], out_sem.at[part]).start()

            @pl.when(part >= nx)
            def _():
                pltpu.make_async_copy(held.at[part], own.at[offset_of(part)], out_sem.at[part]).start()

    for part in range(2 * nx):
        target = sib if part < nx else own
        pltpu.make_async_copy(held.at[part], target.at[(part % nx + 1) % nx], out_sem.at[part]).wait()


def forward_call(g, first, nx, nq, where, tok, masks, weights, after, cost):
    count, depth = tok.shape
    rows = 2 * nx * nq * g
    shape = jax.ShapeDtypeStruct((nx, 4, nq * g, count), jnp.bfloat16)
    return pl.pallas_call(
        functools.partial(forward_kernel, g, first, nx, nq),
        in_specs=[SM, VM, VM, VM] + [HBM] * 4 + [ANY] * len(after),
        out_specs=(ANY, ANY),
        out_shape=(shape, shape),
        scratch_shapes=[
            pltpu.VMEM((SLOTS, 4, g, depth), jnp.bfloat16),
            pltpu.VMEM((2 * nx, 4, nq * g, count), jnp.bfloat16),
            pltpu.SemaphoreType.DMA((SLOTS, 4)),
            pltpu.SemaphoreType.DMA((2 * nx,)),
        ],
        compiler_params=params(44),
        cost_estimate=cost,
        name="forward",
    )(where, tok, *masks, *weights, *after)


def sum_kernel(count, *refs):
    own, got = refs[0], refs[1]
    outs = refs[-count:]
    for k, out in enumerate(outs):
        out[...] = (own[k + 1].astype(jnp.float32) + got[k + 1].astype(jnp.float32)).astype(jnp.bfloat16)


def sum_call(nx, own, got, after):
    shape = own.shape[1:]
    step = min(64, shape[1])
    block = pl.BlockSpec((nx,) + (4, step, shape[2]), lambda i: (0, 0, i, 0))
    out_block = pl.BlockSpec((4, step, shape[2]), lambda i: (0, i, 0))
    size = math.prod(shape)
    return pl.pallas_call(
        functools.partial(sum_kernel, nx - 1),
        grid=(shape[1] // step,),
        in_specs=[block, block] + [ANY] * len(after),
        out_specs=[out_block] * (nx - 1),
        out_shape=[jax.ShapeDtypeStruct(shape, jnp.bfloat16)] * (nx - 1),
        compiler_params=params(16),
        cost_estimate=SHORT,
        name="sums",
    )(own, got, *after)


def delta_kernel(count, own, got, *refs):
    arrived, out = refs[:count], refs[-1]

    def total(m):
        value = own[0, m].astype(jnp.float32) + got[0, m].astype(jnp.float32)
        for ref in arrived:
            value = value + ref[m].astype(jnp.float32)
        return value

    teacher_g, teacher_u, student_g, student_u = total(0), total(1), total(2), total(3)
    sigma_s = jax.nn.sigmoid(student_g)
    sigma_t = jax.nn.sigmoid(teacher_g)
    diff = student_g * sigma_s * student_u - teacher_g * sigma_t * teacher_u
    out[0] = (diff * student_u * sigma_s * (1.0 + student_g * (1.0 - sigma_s))).astype(jnp.bfloat16)
    out[1] = (diff * student_g * sigma_s).astype(jnp.bfloat16)


def delta_call(nx, own, got, arrived, after, cost):
    rows, count = own.shape[2:]
    step = min(64, rows)
    first = pl.BlockSpec((1, 4, step, count), lambda i: (0, 0, i, 0))
    other = pl.BlockSpec((4, step, count), lambda i: (0, i, 0))
    return pl.pallas_call(
        functools.partial(delta_kernel, nx - 1),
        grid=(rows // step,),
        in_specs=[first, first] + [other] * (nx - 1) + [ANY] * len(after),
        out_specs=pl.BlockSpec((2, step, count), lambda i: (0, i, 0)),
        out_shape=jax.ShapeDtypeStruct((2, rows, count), jnp.bfloat16),
        compiler_params=params(16),
        cost_estimate=cost,
        name="deltas",
    )(own, got, *arrived, *after)


def relay_kernel(count, *refs):
    for source, target in zip(refs[:count], refs[-count:]):
        target[...] = source[...]


def relay_call(pieces, after):
    count = len(pieces)
    return pl.pallas_call(
        functools.partial(relay_kernel, count),
        in_specs=[VM] * count + [ANY] * len(after),
        out_specs=[VM] * count,
        out_shape=[jax.ShapeDtypeStruct(x.shape, x.dtype) for x in pieces],
        compiler_params=params(16),
        cost_estimate=SHORT,
        name="relay",
    )(*pieces, *after)


def grads_kernel(g, first, nx, nq, places, width, where, tok, mg, mu, *refs):
    count = len(places)
    deltas = refs[:count]
    gate, up, _, left, buf, in_sem, out_sem = refs[-7:]
    masks, outs = (mg, mu), (gate, up)
    rows = nq * g
    steps = 2 * (tok.shape[1] // width)
    arrivals = [pltpu.make_async_copy(deltas[b], left.at[:, b], in_sem.at[b]) for b in range(count)]
    for copy in arrivals:
        copy.start()

    groups = []
    for other, k in places:
        side = lax.rem(where[0] + other, 2)
        groups.append(first + (side * nx + lax.rem(where[1] + nx - k, nx)) * nq)

    def columns(t):
        return pl.ds(pl.multiple_of((t // 2) * width, width), width)

    def leave(t, m):
        slot = lax.rem(t, OUT_SLOTS)
        return [
            pltpu.make_async_copy(
                buf.at[slot, b],
                outs[m].at[pl.ds(pl.multiple_of(groups[b] * g, g), rows), columns(t)],
                out_sem.at[slot, b],
            )
            for b in range(count)
        ]

    for copy in arrivals:
        copy.wait()

    @pl.loop(0, steps)
    def _(t):
        slot, m, cols = lax.rem(t, OUT_SLOTS), lax.rem(t, 2), columns(t)

        @pl.when(t >= OUT_SLOTS)
        def _():
            for copy in leave(t - OUT_SLOTS, 0):
                copy.wait()

        sums = jnp.dot(
            left[m].reshape(count * rows, left.shape[3]), tok[:, cols], preferred_element_type=jnp.float32
        ).astype(jnp.bfloat16)
        for b in range(count):
            for r in range(nq):
                gate_row = masks[0][groups[b] + r, :, cols]
                up_row = masks[1][groups[b] + r, :, cols]
                row = jnp.where(m == 0, gate_row, up_row).astype(jnp.bfloat16)
                at = b * rows + r * g
                buf[slot, b, r * g : (r + 1) * g] = sums[at : at + g] * row
        for which in range(2):

            @pl.when(m == which)
            def _():
                for copy in leave(t, which):
                    copy.start()

    for t in range(max(0, steps - OUT_SLOTS), steps):
        for copy in leave(t, t % 2):
            copy.wait()


def grads_call(g, first, nx, nq, where, tok, masks, deltas, places, grads, shape, after, cost):
    tokens, depth = tok.shape
    rows = nq * g
    count = len(deltas)
    width = min(512, depth)
    held = [] if grads is None else list(grads)
    base = 4 + count
    grad = jax.ShapeDtypeStruct(shape, jnp.bfloat16)
    return pl.pallas_call(
        functools.partial(grads_kernel, g, first, nx, nq, places, width),
        in_specs=[SM, VM, VM, VM] + [ANY] * count + [HBM] * len(held) + [ANY] * len(after),
        out_specs=(HBM, HBM, ANY),
        out_shape=(grad, grad, jax.ShapeDtypeStruct((8, BLOCK), jnp.float32)),
        scratch_shapes=[
            pltpu.VMEM((2, count, rows, tokens), jnp.bfloat16),
            pltpu.VMEM((OUT_SLOTS, count, rows, width), jnp.bfloat16),
            pltpu.SemaphoreType.DMA((count,)),
            pltpu.SemaphoreType.DMA((OUT_SLOTS, count)),
        ],
        input_output_aliases={base: 0, base + 1: 1} if held else {},
        compiler_params=params(44),
        cost_estimate=cost,
        name="grads",
    )(where, tok, *masks, *deltas, *held, *after)


def per_device(nx, nz, tokens, teacher_gate, teacher_up, student_gate, student_up, keep_gate, keep_up):
    local_ff, local_d = student_gate.shape
    g = math.gcd(local_ff // (2 * nx), BLOCK)
    block_count = local_d // BLOCK
    first_block = lax.axis_index(("col", "sub")) * block_count
    masks = [mask_rows(keep, first_block, block_count, g) for keep in (keep_gate, keep_up)]
    weights = (teacher_gate, teacher_up, student_gate, student_up)
    where = jnp.stack([lax.axis_index("sub"), lax.axis_index("col")]).astype(jnp.int32)

    def swap(x):
        return lax.ppermute(x, "sub", [(0, 1), (1, 0)])

    def turn(x, k):
        return lax.ppermute(x, "col", [(i, (i + k) % nx) for i in range(nx)])

    if nz == 4:
        others = [lax.ppermute(tokens, "grid", [(i, i ^ k) for i in range(nz)]) for k in (1, 2, 3)]
        tok = jnp.concatenate([tokens] + others, axis=0)
    else:
        tok = lax.all_gather(tokens, "grid", axis=0, tiled=True)

    total = local_ff // (2 * nx * g)
    if sum(PARTS) == total:
        parts, order = PARTS, ORDER
    else:
        parts = (1,) * total
        order = [kind + str(u) for u in range(total) for kind in "FSDRG"]
    grads = None
    units = [(sum(parts[:u]) * 2 * nx, nq) for u, nq in enumerate(parts)]
    state = {}
    after = ()
    for step in order:
        kind, u = step[0], int(step[1])
        cost = LONG if step.endswith("+") else SHORT
        first, nq = units[u]
        if kind == "F":
            sib, own = forward_call(g, first, nx, nq, where, tok, masks, weights, after, cost)
            state[u] = (own, swap(sib))
            after = (own,)
        elif kind == "S":
            own, got = state[u]
            sends = sum_call(nx, own, got, after)
            state[u] = (own, got, [turn(sends[k - 1], k) for k in range(1, nx)])
            after = (sends[0],)
        elif kind == "D":
            own, got, arrived = state[u]
            mine = delta_call(nx, own, got, arrived, after, cost)
            state[u] = ([mine, swap(mine)], [turn(mine, k) for k in range(1, nx)])
            after = (mine,)
        elif kind == "R":
            (mine, theirs), far = state[u]
            near = relay_call(far, after)
            state[u] = [mine, *near, theirs, *[swap(x) for x in near]]
            after = (near[0],)
        else:
            near = [k for k in range(nx) if kind == "G" or (k == 0) == (kind == "H")]
            places = tuple((other, k) for other in range(2) for k in near)
            if kind == "H":
                pieces = state[u][0]
            else:
                pieces = [state[u][other * nx + k] for other, k in places]
            *grads, done = grads_call(
                g, first, nx, nq, where, tok, masks, pieces, places, grads, (local_ff, local_d), after, cost
            )
            after = (done,)
    return tuple(grads)


def solution(mesh):
    return jax.shard_map(
        functools.partial(per_device, mesh.shape["col"], mesh.shape["grid"]),
        mesh=mesh,
        in_specs=(
            P(("groups", "grid"), ("col", "sub")),
            P("grid", ("col", "sub")),
            P("grid", ("col", "sub")),
            P("grid", ("col", "sub")),
            P("grid", ("col", "sub")),
            P("grid", None),
            P("grid", None),
        ),
        out_specs=(P(("groups", "grid"), ("col", "sub")), P(("groups", "grid"), ("col", "sub"))),
        check_vma=False,
    )
```
